256 devices in a mesh: tile: 32 (over z, x), zslab: 8 (over y, core).
Axes of the slice: x: 4, y: 4, z: 8, core: 2. Of those that a mesh axis runs over, the one named last changes fastest.
Arguments:
- band: bfloat16 [32, 4, 128, 64, 512], P('tile', None, 'zslab'), may hold values from -6 to 6
- pairs: int32 [64, 4], replicated, may hold values from 0 to 31, as said below
- extents: int32 [64, 2], replicated, may hold values from 32 to 512, as said below
Outputs:
- maps: float32 [64, 128, 32, 256], P('tile', 'zslab')
The draws below stay inside these ranges and needn't reach their ends.
Inputs may be any that keep to these rules, and one draw needn't show every extreme that they name: `pairs`: every slot (tile, face) with tile < 32 and face < 4 is named by exactly one pair, and a pair names two different slots. `extents`: column 0 lies in 32 to 64, column 1 in 256 to 512; some pair has both at their most.
All inputs are finite; a program needn't handle non-finite values.
Results may differ from the reference program's by a relative error of at most 0.012.
The reference program's roundings to bfloat16 on the way count: a program that leaves them out, or rounds other values in their place, can miss the bound.
Values may be sent and summed in bfloat16 or wider, within the bound.
A program may use at most 64 MiB of HBM per device.

```python
import math
import jax
import jax.numpy as jnp
from jax import lax

GX = 32
GY = 256
GZ = 128
FACES = 4
TILES = 32
PAIRS = 64


def draw_pairs(key, part):
    grid_cols = 4
    grid_rows = TILES // grid_cols
    tile_order = jax.random.permutation(jax.random.fold_in(key, 11), TILES).astype(jnp.int32)
    places = jnp.arange(TILES, dtype=jnp.int32)
    grid_row = places // grid_cols
    grid_col = places % grid_cols
    eastern = grid_row * grid_cols + (grid_col + 1) % grid_cols
    southern = (grid_row + 1) % grid_rows * grid_cols + grid_col
    blank = jnp.zeros((TILES,), jnp.int32)
    first_rows = jnp.stack([tile_order, blank, tile_order[eastern], blank + 1], axis=1)
    second_tile_rows = jnp.stack([tile_order, blank + 2, tile_order[southern], blank + 3], axis=1)
    listing = jnp.concatenate([first_rows, second_tile_rows], axis=0)
    shuffle = jax.random.permutation(jax.random.fold_in(key, 12), PAIRS)
    return listing[shuffle].astype(jnp.int32)


def draw_extents(key, part):
    across = jax.random.randint(jax.random.fold_in(key, 21), (PAIRS,), GX, 2 * GX + 1).astype(jnp.int32)
    along = jax.random.randint(jax.random.fold_in(key, 22), (PAIRS,), GY, 2 * GY + 1).astype(jnp.int32)
    across = across.at[0].set(2 * GX).at[1].set(GX)
    along = along.at[0].set(2 * GY).at[1].set(GY)
    return jnp.stack([across, along], axis=1).astype(jnp.int32)


def block_levels(key, extent, shards, low, high):
    def one(axis_at, parts):
        draws = jax.random.uniform(jax.random.fold_in(jax.random.fold_in(key, 6), axis_at), (parts,), jnp.float32, low / len(shards), high / len(shards))
        return jnp.repeat(jnp.exp(draws), extent[axis_at] // parts).reshape((-1,) + (1,) * (len(extent) - axis_at - 1))

    factor_of = one(*shards[0])
    for cut in shards[1:]:
        factor_of = factor_of * one(*cut)
    return factor_of


def noise(own_key, shape, scale, bound, cuts=(), kind=jnp.bfloat16):
    factor_of = block_levels(own_key, shape, cuts, -0.22, 0.18) if cuts else 1.0
    result = jax.random.normal(own_key, shape, jnp.float32) * scale * factor_of
    return jnp.minimum(jnp.maximum(result, -bound), bound).astype(kind)


def setup_inputs(seed: int = 0) -> dict:
    key_of = jax.random.split(jax.random.key(seed), 4)
    return {
        "band": noise(key_of[0], (TILES, FACES, GZ, 2 * GX, 2 * GY), 1.0, 6.0, ((0, 32), (2, 8))),
        "pairs": draw_pairs(jax.random.fold_in(key_of[3], 71), 0),
        "extents": draw_extents(jax.random.fold_in(key_of[3], 71), 0),
    }


def dft_tables(length):
    indices = jnp.arange(length, dtype=jnp.int32)
    modular = indices[:, None] * indices[None, :] % length
    angles = modular.astype(jnp.float32) * (2.0 * math.pi / length)
    factor = 1.0 / math.sqrt(length)
    return ((jnp.cos(angles) * factor).astype(jnp.bfloat16), (jnp.sin(angles) * factor).astype(jnp.bfloat16))

def contract(form, left, right):
    return jnp.einsum(form, left.astype(jnp.float32), right.astype(jnp.float32))

def reduce_resolution(image_volume, crop_bounds):
    row_mask = (jnp.arange(image_volume.shape[2], dtype=jnp.int32)[None, :] < crop_bounds[:, 0:1]).astype(jnp.float32)
    col_mask = (jnp.arange(image_volume.shape[3], dtype=jnp.int32)[None, :] < crop_bounds[:, 1:2]).astype(jnp.float32)
    masked = image_volume.astype(jnp.float32) * row_mask[:, None, :, None] * col_mask[:, None, None, :]
    shaped = masked.reshape(image_volume.shape[0], image_volume.shape[1], GX, 2, GY, 2)
    return (0.5 * lax.optimization_barrier(jnp.sum(shaped, axis=(3, 5)))).astype(jnp.bfloat16)

def reference(band, pairs, extents):
    tables_x = dft_tables(GX)
    tables_y = dft_tables(GY)
    tables_z = dft_tables(GZ)
    first_slot = pairs[:, 0] * FACES + pairs[:, 1]
    second_slot = pairs[:, 2] * FACES + pairs[:, 3]
    slot_ext = jnp.zeros((TILES * FACES, 2), jnp.int32).at[first_slot].set(extents).at[second_slot].set(extents)
    slot_ext = slot_ext.reshape(TILES, FACES, 2)

    def forward(einsum_inputs):
        reduced_volume = reduce_resolution(einsum_inputs[0], einsum_inputs[1])
        y_re = contract('fzxy,yk->fzxk', reduced_volume, tables_y[0]).astype(jnp.bfloat16)
        y_im = (-contract('fzxy,yk->fzxk', reduced_volume, tables_y[1])).astype(jnp.bfloat16)
        x_re = (contract('fzxk,xj->fzjk', y_re, tables_x[0]) + contract('fzxk,xj->fzjk', y_im, tables_x[1])).astype(jnp.bfloat16)
        x_im = (contract('fzxk,xj->fzjk', y_im, tables_x[0]) - contract('fzxk,xj->fzjk', y_re, tables_x[1])).astype(jnp.bfloat16)
        z_re = (contract('fzjk,zm->fmjk', x_re, tables_z[0]) + contract('fzjk,zm->fmjk', x_im, tables_z[1])).astype(jnp.bfloat16)
        z_im = (contract('fzjk,zm->fmjk', x_im, tables_z[0]) - contract('fzjk,zm->fmjk', x_re, tables_z[1])).astype(jnp.bfloat16)
        return (z_re, z_im)
    spec_re, spec_im = lax.map(forward, (band, slot_ext))

    def correlate(entry):
        first_re = spec_re[entry[0], entry[1]].astype(jnp.float32)
        first_im = spec_im[entry[0], entry[1]].astype(jnp.float32)
        second_re = spec_re[entry[2], entry[3]].astype(jnp.float32)
        second_im = spec_im[entry[2], entry[3]].astype(jnp.float32)
        cross_re = first_re * second_re + first_im * second_im
        cross_im = first_im * second_re - first_re * second_im
        scaled = jnp.sqrt(cross_re * cross_re + cross_im * cross_im + 1.0)
        phase_real_part = (cross_re / scaled).astype(jnp.bfloat16)
        phase_im = (cross_im / scaled).astype(jnp.bfloat16)
        w_re = (contract('mjk,mz->zjk', phase_real_part, tables_z[0]) - contract('mjk,mz->zjk', phase_im, tables_z[1])).astype(jnp.bfloat16)
        w_im = (contract('mjk,mz->zjk', phase_im, tables_z[0]) + contract('mjk,mz->zjk', phase_real_part, tables_z[1])).astype(jnp.bfloat16)
        v_re = (contract('zjk,jx->zxk', w_re, tables_x[0]) - contract('zjk,jx->zxk', w_im, tables_x[1])).astype(jnp.bfloat16)
        v_im = (contract('zjk,jx->zxk', w_im, tables_x[0]) + contract('zjk,jx->zxk', w_re, tables_x[1])).astype(jnp.bfloat16)
        return contract('zxk,ky->zxy', v_re, tables_y[0]) - contract('zxk,ky->zxy', v_im, tables_y[1])
    return lax.map(correlate, pairs)
```

```python
import functools
import math

import jax
import jax.numpy as jnp
import ml_dtypes
import numpy as np
from jax import lax
from jax.experimental import pallas as pl
from jax.experimental.pallas import tpu as pltpu
from jax.sharding import PartitionSpec as P

GX, GY, GZ, FACES = 32, 256, 128, 4
HALF = GY // 2
MESH = pl.DeviceIdType.MESH
BF = jnp.bfloat16
F32 = jnp.float32


def dft_tables(length):
    indices = np.arange(length, dtype=np.int64)
    modular = indices[:, None] * indices[None, :] % length
    angles = modular.astype(np.float32) * np.float32(2.0 * math.pi / length)
    factor = np.float32(1.0 / math.sqrt(length))
    return tuple(
        (f(angles) * factor).astype(ml_dtypes.bfloat16).astype(np.float32)
        for f in (np.cos, np.sin)
    )


def complex_forward(c, s):
    m = np.zeros((c.shape[0], 2, c.shape[1], 2), np.float32)
    m[:, 0, :, 0], m[:, 0, :, 1] = c, s
    m[:, 1, :, 1], m[:, 1, :, 0] = c, -s
    return m


def real_pair_forward(c, s):
    n = c.shape[0]
    m = np.zeros((n, 2, n, 2), np.float32)
    for part in (0, 1):
        base = part * (n // 2)
        m[base, 0, :, part], m[base, 1, :, part] = c[0], c[n // 2]
        m[base + 1 : base + n // 2, 0, :, part] = c[1 : n // 2]
        m[base + 1 : base + n // 2, 1, :, part] = -s[1 : n // 2]
    return m


def line_pair_forward(c, s):
    n = c.shape[0]
    m = real_pair_forward(c, s)
    m[0], m[n // 2] = 0.0, 0.0
    for part in (0, 1):
        m[0, part, :, part] = c[0]
        m[n // 2, part, :, part] = c[n // 2]
    return m


def complex_inverse(c, s):
    m = np.zeros((c.shape[0], 2, c.shape[1], 2), np.float32)
    m[:, 0, :, 0], m[:, 0, :, 1] = c, -s
    m[:, 1, :, 1], m[:, 1, :, 0] = c, s
    return m


def doubled(forward):
    m = np.transpose(forward, (2, 3, 0, 1)).copy()
    n = m.shape[2]
    m[:, :, 1 : n // 2] *= 2.0
    m[:, :, n // 2 + 1 :] *= 2.0
    return m


@functools.cache
def constants():
    cx, sx = dft_tables(GX)
    cy, sy = dft_tables(GY)
    cz, sz = dft_tables(GZ)
    to_y = np.concatenate([cy[:, :HALF], -sy[:, :HALF]], axis=1)
    to_y[:, HALF] = cy[:, HALF]
    pool = np.repeat(0.5 * np.eye(GY, dtype=np.float32), 2, axis=0)
    eye4, eye8 = np.eye(4, dtype=np.float32), np.eye(8, dtype=np.float32)

    split = np.zeros((2, 4, GX, 4, GX, 2), np.float32)
    for parity in (0, 1):
        split[parity, ..., parity] = np.einsum("zw,xv->zxwv", eye4, np.eye(GX, dtype=np.float32))

    def x_forward(m):
        return np.einsum("kpxq,zw->kpzqwx", m, eye4).reshape(256, 256)

    def z_forward(m):
        m = m.reshape(32, 4, 2, 8, 4, 4, 2)
        return np.transpose(m, (0, 2, 1, 3, 4, 6, 5)).reshape(256, 256)

    def z_inverse(m):
        m = m.reshape(8, 4, 4, 2, 32, 4, 2)
        return np.transpose(m, (0, 1, 3, 2, 4, 6, 5)).reshape(256, 256)

    def x_inverse(m):
        e = eye8.reshape(8, 2, 4)
        return np.einsum("xpkq,zgw->pzxkgqw", m, e).reshape(512, 512)

    from_y = np.concatenate([2.0 * cy[:HALF], -2.0 * sy[:HALF]], axis=0)
    from_y[0], from_y[HALF] = cy[0], cy[HALF]
    z_line = line_pair_forward(cz, sz)
    x_line = real_pair_forward(cx, sx)
    tables = (
        split.reshape(256, 256),
        pool,
        to_y,
        x_forward(complex_forward(cx, sx)),
        x_forward(x_line),
        z_forward(complex_forward(cz, sz)),
        z_forward(z_line),
        z_inverse(complex_inverse(cz, sz)),
        z_inverse(doubled(z_line)),
        x_inverse(complex_inverse(cx, sx)),
        x_inverse(doubled(x_line)),
        from_y,
    )
    return tuple(t.astype(ml_dtypes.bfloat16) for t in tables)


def dot(a, b):
    return jnp.dot(a, b, preferred_element_type=F32)


def body(tiles, slabs, *refs):
    (pairs_s, pairs_v, extents_v, band, *rest) = refs
    hbm_tables, rest = rest[:12], rest[12:]
    out, rest = rest[0], rest[1:]
    raw, rest = rest[0], rest[1:]
    tables, rest = rest[:12], rest[12:]
    s1, r1, s2, r2, s3, r3, s4, r4, raw_sem, table_sem, *sems = rest
    send1, recv1, send2, recv2, send3, recv3, send4, recv4 = sems
    split, pool, to_y, xf, xf0, zf, zf0, zi, zi0, xi, xi0, from_y = tables
    t = lax.axis_index("tile")
    s = lax.axis_index("zslab")

    barrier = pltpu.get_barrier_semaphore()

    @pl.loop(1, slabs)
    def _(i):
        pl.semaphore_signal(
            barrier, inc=1, device_id=(t, lax.rem(s + i, slabs)), device_id_type=MESH
        )

    @pl.loop(1, tiles)
    def _(i):
        pl.semaphore_signal(
            barrier, inc=1, device_id=(lax.rem(t + i, tiles), s), device_id_type=MESH
        )

    for f in range(FACES):
        pltpu.make_async_copy(band.at[f], raw.at[f], raw_sem.at[f]).start()
    for i in range(12):
        pltpu.make_async_copy(hbm_tables[i], tables[i], table_sem.at[i]).start()

    def table_wait(*which):
        for i in which:
            pltpu.make_async_copy(hbm_tables[i], tables[i], table_sem.at[i]).wait()

    def slab_send(src, dst, send_sem, recv_sem):
        @pl.loop(1, slabs)
        def _(i):
            d = lax.rem(s + i, slabs)
            pltpu.make_async_remote_copy(
                src_ref=src.at[d],
                dst_ref=dst.at[s],
                send_sem=send_sem,
                recv_sem=recv_sem,
                device_id=(t, d),
                device_id_type=MESH,
            ).start()

        pltpu.make_async_copy(src.at[s], dst.at[s], recv_sem).start()

    def tile_send(src, dst, send_sem, recv_sem):
        @pl.loop(1, tiles)
        def _(i):
            d = lax.rem(t + i, tiles)
            pltpu.make_async_remote_copy(
                src_ref=src.at[d],
                dst_ref=dst.at[t],
                send_sem=send_sem,
                recv_sem=recv_sem,
                device_id=(d, s),
                device_id_type=MESH,
            ).start()

        pltpu.make_async_copy(src.at[t], dst.at[t], recv_sem).start()

    def wait_for(ref, sem):
        pltpu.make_async_copy(ref, ref, sem).wait()

    lane0 = lax.broadcasted_iota(jnp.int32, (256, 128), 1) == 0
    two_lane0 = lax.broadcasted_iota(jnp.int32, (256, 256), 1) % 128 == 0
    mixed_line = (s == 0) | (s == slabs // 2)

    first = pairs_v[:, 0:1] * FACES + pairs_v[:, 1:2]
    second = pairs_v[:, 2:3] * FACES + pairs_v[:, 3:4]
    y_rows = lax.broadcasted_iota(jnp.int32, (512, 256), 0)
    x_lanes = lax.broadcasted_iota(jnp.int32, (256, 256), 1) % 64

    table_wait(0, 1, 2, 3, 4)

    def to_x(f, carry):
        slot = t * FACES + f
        named = (first == slot) | (second == slot)
        ex = jnp.sum(jnp.where(named, extents_v[:, 0:1], 0), axis=0, keepdims=True)
        ey = jnp.sum(jnp.where(named, extents_v[:, 1:2], 0), axis=0, keepdims=True)
        y_pool = jnp.where(y_rows < ey, pool[...].astype(F32), 0.0).astype(BF)
        x_split = jnp.where(x_lanes < ex, split[...].astype(F32), 0.0).astype(BF)
        pltpu.make_async_copy(band.at[f], raw.at[f], raw_sem.at[f]).wait()
        parts = []
        for half in range(2):
            y = []
            for g in range(2):
                rows = raw[f, pl.ds(512 * half + 256 * g, 256), :]
                parted = dot(x_split, rows).astype(BF)
                down = (dot(parted[:128], y_pool) + dot(parted[128:], y_pool)).astype(BF)
                y.append(dot(down, to_y[...]).astype(BF))
            stacked = jnp.concatenate(
                [
                    jnp.concatenate([y[0][:, :128], y[1][:, :128]], axis=1),
                    jnp.concatenate([y[0][:, 128:], y[1][:, 128:]], axis=1),
                ],
                axis=0,
            )
            x = jnp.where(two_lane0, dot(xf0[...], stacked), dot(xf[...], stacked))
            parts += [x[:, :128].reshape(32, 8, 128), x[:, 128:].reshape(32, 8, 128)]
        whole = jnp.concatenate(parts, axis=1).astype(BF)
        s1[f] = whole.reshape(slabs, 4, 32, 128)
        return carry

    lax.fori_loop(0, FACES, to_x, 0)

    pl.semaphore_wait(barrier, slabs - 1 + tiles - 1)
    for f in range(FACES):
        slab_send(s1.at[f], r1.at[f], send1.at[f], recv1.at[f])

    table_wait(5, 6, 7, 8, 9, 10, 11)
    zf0[...] = jnp.where(mixed_line, zf0[...].astype(F32), zf[...].astype(F32)).astype(BF)
    zi0[...] = jnp.where(mixed_line, zi0[...].astype(F32), zi[...].astype(F32)).astype(BF)

    def to_z(f, carry):
        wait_for(r1.at[f], recv1.at[f])
        parts = []
        for k in range(4):
            block = r1[f, :, k].reshape(256, 128)
            z = dot(zf[...], block)
            if k == 0:
                z = jnp.where(lane0, dot(zf0[...], block), z)
            parts.append(z.reshape(tiles, 8, 128))
        s2[f] = jnp.concatenate(parts, axis=1).astype(BF)
        tile_send(s2.at[f], r2.at[f], send2.at[f], recv2.at[f])
        return carry

    lax.fori_loop(0, FACES, to_z, 0)

    for f in range(FACES):
        wait_for(r2.at[f], recv2.at[f])
    row = lax.broadcasted_iota(jnp.int32, (8, 128), 0)
    lane = lax.broadcasted_iota(jnp.int32, (8, 128), 1)
    mixed_here = mixed_line & ((t == 0) | (t == tiles // 2))
    two_reals = (lane == 0) & (lax.rem(row, 4) == 0) & mixed_here
    real_row = row < 4

    for q in range(2):

        def correlate(i, carry):
            d = lax.rem(t + i, tiles)
            p = 2 * d + q
            a = r2[pairs_s[p, 1], pairs_s[p, 0]].astype(F32)
            b = r2[pairs_s[p, 3], pairs_s[p, 2]].astype(F32)
            parts = []
            for k in range(4):
                ak, bk = a[8 * k : 8 * k + 8], b[8 * k : 8 * k + 8]
                same = ak * bk
                turned = pltpu.roll(ak, 4, axis=0) * bk
                cross = jnp.where(
                    real_row,
                    same + pltpu.roll(same, 4, axis=0),
                    pltpu.roll(turned, 4, axis=0) - turned,
                )
                if k == 0:
                    cross = jnp.where(two_reals, same, cross)
                square = cross * cross
                total = square + pltpu.roll(square, 4, axis=0)
                if k == 0:
                    total = jnp.where(two_reals, square, total)
                parts.append(cross * lax.rsqrt(total + 1.0))
            s3[q, d] = jnp.concatenate(parts, axis=0).astype(BF)
            return carry

        lax.fori_loop(0, tiles, correlate, 0)
        tile_send(s3.at[q], r3.at[q], send3.at[q], recv3.at[q])

    def from_z(q, carry):
        wait_for(r3.at[q], recv3.at[q])
        got = r3[q].astype(F32)
        for k in range(4):
            block = got[:, 8 * k : 8 * k + 8].reshape(256, 128).astype(BF)
            w = dot(zi[...], block)
            if k == 0:
                w = jnp.where(lane0, dot(zi0[...], block), w)
            s4[q, :, k] = w.astype(BF).reshape(slabs, 32, 128)
        slab_send(s4.at[q], r4.at[q], send4.at[q], recv4.at[q])
        return carry

    lax.fori_loop(0, 2, from_z, 0)

    def from_x(q, carry):
        wait_for(r4.at[q], recv4.at[q])
        for half in range(2):
            block = r4[q, :, :, pl.ds(16 * half, 16), :].reshape(512, 128)
            v = dot(xi[...], block)
            v0 = dot(xi0[...], block)
            re = jnp.where(lane0, v0[:256], v[:256]).astype(BF)
            im = jnp.where(lane0, v0[256:], v[256:]).astype(BF)
            out[q, pl.ds(256 * half, 256), :] = dot(
                jnp.concatenate([re, im], axis=1), from_y[...]
            )
        return carry

    lax.fori_loop(0, 2, from_x, 0)

    for f in range(FACES):
        wait_for(s1.at[f, pl.ds(0, slabs - 1)], send1.at[f])
        wait_for(s2.at[f, pl.ds(0, tiles - 1)], send2.at[f])
    for q in range(2):
        wait_for(s3.at[q, pl.ds(0, tiles - 1)], send3.at[q])
        wait_for(s4.at[q, pl.ds(0, slabs - 1)], send4.at[q])


def solution(mesh):
    tiles, slabs = mesh.shape["tile"], mesh.shape["zslab"]

    def shards(band, pairs, extents):
        tables = constants()
        vmem = pl.BlockSpec(memory_space=pltpu.VMEM)
        smem = pl.BlockSpec(memory_space=pltpu.SMEM)
        anywhere = pl.BlockSpec(memory_space=pl.ANY)
        dma = pltpu.SemaphoreType.DMA
        scratch = [pltpu.VMEM((FACES, 1024, 512), BF)]
        scratch += [pltpu.VMEM(c.shape, BF) for c in tables]
        scratch += [pltpu.VMEM((FACES, slabs, 4, 32, 128), BF)] * 2
        scratch += [pltpu.VMEM((FACES, tiles, 32, 128), BF)] * 2
        scratch += [pltpu.VMEM((2, tiles, 32, 128), BF)] * 2
        scratch += [pltpu.VMEM((2, slabs, 4, 32, 128), BF)] * 2
        scratch += [dma((FACES,)), dma((12,))]
        scratch += [dma((FACES,))] * 4 + [dma((2,))] * 4
        maps = pl.pallas_call(
            functools.partial(body, tiles, slabs),
            out_shape=jax.ShapeDtypeStruct((2, 512, 256), F32),
            in_specs=[smem, vmem, vmem, anywhere] + [anywhere] * 12,
            out_specs=vmem,
            scratch_shapes=scratch,
            compiler_params=pltpu.CompilerParams(
                collective_id=0, has_side_effects=True, vmem_limit_bytes=48 << 20
            ),
        )(pairs, pairs, extents, band.reshape(FACES, 1024, 512), *tables)
        return maps.reshape(2, 16, GX, GY)

    placed = (P("tile", None, "zslab", None, None), P(), P())
    return jax.shard_map(
        shards,
        mesh=mesh,
        in_specs=placed,
        out_specs=P("tile", "zslab", None, None),
        check_vma=False,
    )
```

```python
import functools
import math

import jax
import jax.numpy as jnp
import ml_dtypes
import numpy as np
from jax import lax
from jax.experimental import pallas as pl
from jax.experimental.pallas import tpu as pltpu
from jax.sharding import PartitionSpec as P

GX, GY, GZ, FACES = 32, 256, 128, 4
HALF = GY // 2
VLIM = 52 << 20
MESH = pl.DeviceIdType.MESH
TABLE_ROWS = (256, 512, 256, 256, 256, 256, 256, 256, 256, 1024, 1024, 256)
FIRST_ROWS = sum(TABLE_ROWS[:5])
LATER_ROWS = sum(TABLE_ROWS[5:])
BF = jnp.bfloat16
F32 = jnp.float32


def dft_tables(length):
    indices = np.arange(length, dtype=np.int64)
    modular = indices[:, None] * indices[None, :] % length
    angles = modular.astype(np.float32) * np.float32(2.0 * math.pi / length)
    factor = np.float32(1.0 / math.sqrt(length))
    return tuple(
        (f(angles) * factor).astype(ml_dtypes.bfloat16).astype(np.float32)
        for f in (np.cos, np.sin)
    )


def complex_forward(c, s):
    m = np.zeros((c.shape[0], 2, c.shape[1], 2), np.float32)
    m[:, 0, :, 0], m[:, 0, :, 1] = c, s
    m[:, 1, :, 1], m[:, 1, :, 0] = c, -s
    return m


def real_pair_forward(c, s):
    n = c.shape[0]
    m = np.zeros((n, 2, n, 2), np.float32)
    for part in (0, 1):
        base = part * (n // 2)
        m[base, 0, :, part], m[base, 1, :, part] = c[0], c[n // 2]
        m[base + 1 : base + n // 2, 0, :, part] = c[1 : n // 2]
        m[base + 1 : base + n // 2, 1, :, part] = -s[1 : n // 2]
    return m


def line_pair_forward(c, s):
    n = c.shape[0]
    m = real_pair_forward(c, s)
    m[0], m[n // 2] = 0.0, 0.0
    for part in (0, 1):
        m[0, part, :, part] = c[0]
        m[n // 2, part, :, part] = c[n // 2]
    return m


def complex_inverse(c, s):
    m = np.zeros((c.shape[0], 2, c.shape[1], 2), np.float32)
    m[:, 0, :, 0], m[:, 0, :, 1] = c, -s
    m[:, 1, :, 1], m[:, 1, :, 0] = c, s
    return m


def doubled(forward):
    m = np.transpose(forward, (2, 3, 0, 1)).copy()
    n = m.shape[2]
    m[:, :, 1 : n // 2] *= 2.0
    m[:, :, n // 2 + 1 :] *= 2.0
    return m


@functools.cache
def constants():
    cx, sx = dft_tables(GX)
    cy, sy = dft_tables(GY)
    cz, sz = dft_tables(GZ)
    to_y = np.concatenate([cy[:, :HALF], -sy[:, :HALF]], axis=1)
    to_y[:, HALF] = cy[:, HALF]
    pool = np.repeat(0.5 * np.eye(GY, dtype=np.float32), 2, axis=0)
    eye4, eye8 = np.eye(4, dtype=np.float32), np.eye(8, dtype=np.float32)

    split = np.zeros((2, 4, GX, 4, GX, 2), np.float32)
    for parity in (0, 1):
        split[parity, ..., parity] = np.einsum("zw,xv->zxwv", eye4, np.eye(GX, dtype=np.float32))

    def x_forward(m):
        return np.einsum("kpxq,zw->kpzqwx", m, eye4).reshape(256, 256)

    def z_forward(m):
        m = m.reshape(32, 4, 2, 8, 4, 4, 2)
        return np.transpose(m, (0, 2, 1, 3, 4, 6, 5)).reshape(256, 256)

    def z_inverse(m):
        m = m.reshape(8, 4, 4, 2, 32, 4, 2)
        return np.transpose(m, (0, 1, 3, 2, 4, 6, 5)).reshape(256, 256)

    def x_inverse(m):
        e = eye8.reshape(8, 2, 4)
        return np.einsum("xpkq,zgw->pzxkgqw", m, e).reshape(512, 512)

    from_y = np.concatenate([2.0 * cy[:HALF], -2.0 * sy[:HALF]], axis=0)
    from_y[0], from_y[HALF] = cy[0], cy[HALF]
    z_line = line_pair_forward(cz, sz)
    x_line = real_pair_forward(cx, sx)
    tables = (
        split.reshape(256, 256),
        pool,
        to_y,
        x_forward(complex_forward(cx, sx)),
        x_forward(x_line),
        z_forward(complex_forward(cz, sz)),
        z_forward(z_line),
        z_inverse(complex_inverse(cz, sz)),
        z_inverse(doubled(z_line)),
        x_inverse(complex_inverse(cx, sx)),
        x_inverse(doubled(x_line)),
        from_y,
    )
    tables = [t.reshape(-1, 256) if t.shape[1] == 256 else np.concatenate([t[:, :256], t[:, 256:]]) for t in tables]
    return np.concatenate(tables).astype(ml_dtypes.bfloat16)


def dot(a, b):
    return jnp.dot(a, b, preferred_element_type=F32)


def body(tiles, slabs, *refs):
    (pairs_s, pairs_hbm, extents_hbm, band, hbm_tables, out, raw, tables, pairs_v, extents_v, *rest) = refs
    s1, r1, s2, r2, s3, r3, s4, r4, raw_sem, table_sem, *sems = rest
    send1, recv1, send2, recv2, send3, recv3, send4, recv4 = sems
    at, views = 0, []
    for rows in TABLE_ROWS:
        views.append(tables.at[pl.ds(at, rows)])
        at += rows
    split, pool, to_y, xf, xf0, zf, zf0, zi, zi0, xi, xi0, from_y = views
    t = lax.axis_index("tile")
    s = lax.axis_index("zslab")

    barrier = pltpu.get_barrier_semaphore()

    @pl.loop(1, slabs)
    def _(i):
        pl.semaphore_signal(
            barrier, inc=1, device_id=(t, lax.rem(s + i, slabs)), device_id_type=MESH
        )

    @pl.loop(1, tiles)
    def _(i):
        pl.semaphore_signal(
            barrier, inc=1, device_id=(lax.rem(t + i, tiles), s), device_id_type=MESH
        )

    fetches = [
        pltpu.make_async_copy(
            hbm_tables.at[pl.ds(0, FIRST_ROWS)], tables.at[pl.ds(0, FIRST_ROWS)], table_sem.at[0]
        ),
        pltpu.make_async_copy(pairs_hbm, pairs_v, table_sem.at[1]),
        pltpu.make_async_copy(extents_hbm, extents_v, table_sem.at[2]),
    ]
    later = pltpu.make_async_copy(
        hbm_tables.at[pl.ds(FIRST_ROWS, LATER_ROWS)],
        tables.at[pl.ds(FIRST_ROWS, LATER_ROWS)],
        table_sem.at[3],
    )
    for fetch in fetches:
        fetch.start()
    for f in range(FACES):
        pltpu.make_async_copy(band.at[f], raw.at[f], raw_sem.at[f]).start()
    later.start()

    def slab_send(src, dst, send_sem, recv_sem):
        @pl.loop(1, slabs)
        def _(i):
            d = lax.rem(s + i, slabs)
            pltpu.make_async_remote_copy(
                src_ref=src.at[d],
                dst_ref=dst.at[s],
                send_sem=send_sem,
                recv_sem=recv_sem,
                device_id=(t, d),
                device_id_type=MESH,
            ).start()

        pltpu.make_async_copy(src.at[s], dst.at[s], recv_sem).start()

    def tile_send(src, dst, send_sem, recv_sem):
        @pl.loop(1, tiles)
        def _(i):
            d = lax.rem(t + i, tiles)
            pltpu.make_async_remote_copy(
                src_ref=src.at[d],
                dst_ref=dst.at[t],
                send_sem=send_sem,
                recv_sem=recv_sem,
                device_id=(d, s),
                device_id_type=MESH,
            ).start()

        pltpu.make_async_copy(src.at[t], dst.at[t], recv_sem).start()

    def wait_for(ref, sem):
        pltpu.make_async_copy(ref, ref, sem).wait()

    lane0 = lax.broadcasted_iota(jnp.int32, (256, 128), 1) == 0
    two_lane0 = lax.broadcasted_iota(jnp.int32, (256, 256), 1) % 128 == 0
    mixed_line = (s == 0) | (s == slabs // 2)

    for fetch in fetches:
        fetch.wait()
    first = pairs_v[0:1] * FACES + pairs_v[1:2]
    second = pairs_v[2:3] * FACES + pairs_v[3:4]
    y_rows = lax.broadcasted_iota(jnp.int32, (512, 256), 0)
    x_lanes = lax.broadcasted_iota(jnp.int32, (256, 256), 1) % 64


    def to_x(f):
        slot = t * FACES + f
        named = (first == slot) | (second == slot)
        ex = jnp.sum(jnp.where(named, extents_v[0:1], 0), axis=1, keepdims=True)
        ey = jnp.sum(jnp.where(named, extents_v[1:2], 0), axis=1, keepdims=True)
        y_pool = jnp.where(y_rows < ey, pool[...].astype(F32), 0.0).astype(BF)
        x_split = jnp.where(x_lanes < ex, split[...].astype(F32), 0.0).astype(BF)
        pltpu.make_async_copy(band.at[f], raw.at[f], raw_sem.at[f]).wait()
        parts = []
        for half in range(2):
            y = []
            for g in range(2):
                rows = raw[f, pl.ds(512 * half + 256 * g, 256), :]
                parted = dot(x_split, rows).astype(BF)
                down = (dot(parted[:128], y_pool) + dot(parted[128:], y_pool)).astype(BF)
                y.append(dot(down, to_y[...]).astype(BF))
            stacked = jnp.concatenate(
                [
                    jnp.concatenate([y[0][:, :128], y[1][:, :128]], axis=1),
                    jnp.concatenate([y[0][:, 128:], y[1][:, 128:]], axis=1),
                ],
                axis=0,
            )
            x = jnp.where(two_lane0, dot(xf0[...], stacked), dot(xf[...], stacked))
            parts += [x[:, :128].reshape(32, 8, 128), x[:, 128:].reshape(32, 8, 128)]
        whole = jnp.concatenate(parts, axis=1).astype(BF)
        s1[f] = whole.reshape(slabs, 4, 32, 128)

    def mix_tables():
        later.wait()
        zf0[...] = jnp.where(mixed_line, zf0[...].astype(F32), zf[...].astype(F32)).astype(BF)
        zi0[...] = jnp.where(mixed_line, zi0[...].astype(F32), zi[...].astype(F32)).astype(BF)

    def to_z(f):
        wait_for(r1.at[f], recv1.at[f])

        parts = []
        for k in range(4):
            block = r1[f, :, k].reshape(256, 128)
            z = dot(zf[...], block)
            if k == 0:
                z = jnp.where(lane0, dot(zf0[...], block), z)
            parts.append(z.reshape(tiles, 8, 128))
        s2[f] = jnp.concatenate(parts, axis=1).astype(BF)
        tile_send(s2.at[f], r2.at[f], send2.at[f], recv2.at[f])

    def forward(i, carry):
        @pl.when(i < FACES)
        def _():
            to_x(i)

            @pl.when(i == 0)
            def _():
                pl.semaphore_wait(barrier, slabs - 1 + tiles - 1)

            slab_send(s1.at[i], r1.at[i], send1.at[i], recv1.at[i])

            @pl.when(i == 0)
            def _():
                mix_tables()

        @pl.when(i > 0)
        def _():
            to_z(i - 1)

        return carry

    lax.fori_loop(0, FACES + 1, forward, 0)

    for f in range(FACES):
        wait_for(r2.at[f], recv2.at[f])
    row = lax.broadcasted_iota(jnp.int32, (8, 128), 0)
    lane = lax.broadcasted_iota(jnp.int32, (8, 128), 1)
    mixed_here = mixed_line & ((t == 0) | (t == tiles // 2))
    two_reals = (lane == 0) & (lax.rem(row, 4) == 0) & mixed_here
    real_row = row < 4

    for q in range(2):

        def correlate(i, carry):
            d = lax.rem(t + i, tiles)
            p = 2 * d + q
            a = r2[pairs_s[1, p], pairs_s[0, p]].astype(F32)
            b = r2[pairs_s[3, p], pairs_s[2, p]].astype(F32)
            parts = []
            for k in range(4):
                ak, bk = a[8 * k : 8 * k + 8], b[8 * k : 8 * k + 8]
                same = ak * bk
                turned = pltpu.roll(ak, 4, axis=0) * bk
                cross = jnp.where(
                    real_row,
                    same + pltpu.roll(same, 4, axis=0),
                    pltpu.roll(turned, 4, axis=0) - turned,
                )
                if k == 0:
                    cross = jnp.where(two_reals, same, cross)
                square = cross * cross
                total = square + pltpu.roll(square, 4, axis=0)
                if k == 0:
                    total = jnp.where(two_reals, square, total)
                parts.append(cross * lax.rsqrt(total + 1.0))
            s3[q, d] = jnp.concatenate(parts, axis=0).astype(BF)

            @pl.when(i < tiles)
            def _():
                pltpu.make_async_remote_copy(
                    src_ref=s3.at[q, d],
                    dst_ref=r3.at[q, t],
                    send_sem=send3.at[q],
                    recv_sem=recv3.at[q],
                    device_id=(d, s),
                    device_id_type=MESH,
                ).start()

            return carry

        lax.fori_loop(1, tiles + 1, correlate, 0)
        pltpu.make_async_copy(s3.at[q, t], r3.at[q, t], recv3.at[q]).start()

    def from_z(q, carry):
        wait_for(r3.at[q], recv3.at[q])
        got = r3[q].astype(F32)
        for k in range(4):
            block = got[:, 8 * k : 8 * k + 8].reshape(256, 128).astype(BF)
            w = dot(zi[...], block)
            if k == 0:
                w = jnp.where(lane0, dot(zi0[...], block), w)
            s4[q, :, k] = w.astype(BF).reshape(slabs, 32, 128)
        slab_send(s4.at[q], r4.at[q], send4.at[q], recv4.at[q])
        return carry

    lax.fori_loop(0, 2, from_z, 0)

    def from_x(q, carry):
        wait_for(r4.at[q], recv4.at[q])
        for half in range(2):
            block = r4[q, :, :, pl.ds(16 * half, 16), :].reshape(512, 128)
            v = dot(xi[:512], block[:256]) + dot(xi[512:], block[256:])
            v0 = dot(xi0[:512], block[:256]) + dot(xi0[512:], block[256:])
            re = jnp.where(lane0, v0[:256], v[:256]).astype(BF)
            im = jnp.where(lane0, v0[256:], v[256:]).astype(BF)
            out[q, pl.ds(256 * half, 256), :] = dot(
                jnp.concatenate([re, im], axis=1), from_y[...]
            )
        return carry

    lax.fori_loop(0, 2, from_x, 0)

    for f in range(FACES):
        wait_for(s1.at[f, pl.ds(0, slabs - 1)], send1.at[f])
        wait_for(s2.at[f, pl.ds(0, tiles - 1)], send2.at[f])
    for q in range(2):
        wait_for(s3.at[q, pl.ds(0, tiles - 1)], send3.at[q])
        wait_for(s4.at[q, pl.ds(0, slabs - 1)], send4.at[q])


def solution(mesh):
    tiles, slabs = mesh.shape["tile"], mesh.shape["zslab"]

    def shards(band, pairs, extents):
        tables = constants()
        vmem = pl.BlockSpec(memory_space=pltpu.VMEM)
        smem = pl.BlockSpec(memory_space=pltpu.SMEM)
        anywhere = pl.BlockSpec(memory_space=pl.ANY)
        dma = pltpu.SemaphoreType.DMA
        scratch = [pltpu.VMEM((FACES, 1024, 512), BF)]
        scratch += [pltpu.VMEM(tables.shape, BF)]
        scratch += [pltpu.VMEM((4, 64), jnp.int32), pltpu.VMEM((2, 64), jnp.int32)]
        scratch += [pltpu.VMEM((FACES, slabs, 4, 32, 128), BF)] * 2
        scratch += [pltpu.VMEM((FACES, tiles, 32, 128), BF)] * 2
        scratch += [pltpu.VMEM((2, tiles, 32, 128), BF)] * 2
        scratch += [pltpu.VMEM((2, slabs, 4, 32, 128), BF)] * 2
        scratch += [dma((FACES,)), dma((4,))]
        scratch += [dma((FACES,))] * 4 + [dma((2,))] * 4
        maps = pl.pallas_call(
            functools.partial(body, tiles, slabs),
            out_shape=jax.ShapeDtypeStruct((2, 512, 256), F32),
            in_specs=[smem] + [anywhere] * 4,
            out_specs=vmem,
            scratch_shapes=scratch,
            compiler_params=pltpu.CompilerParams(
                collective_id=0, has_side_effects=True, vmem_limit_bytes=VLIM
            ),
        )(pairs.T, pairs.T, extents.T, band.reshape(FACES, 1024, 512), tables)
        return maps.reshape(2, 16, GX, GY)

    placed = (P("tile", None, "zslab", None, None), P(), P())
    return jax.shard_map(
        shards,
        mesh=mesh,
        in_specs=placed,
        out_specs=P("tile", "zslab", None, None),
        check_vma=False,
    )
```

```python
import functools
import math

import jax
import jax.numpy as jnp
import ml_dtypes
import numpy as np
from jax import lax
from jax.experimental import pallas as pl
from jax.experimental.pallas import tpu as pltpu
from jax.sharding import PartitionSpec as P

GX, GY, GZ, FACES = 32, 256, 128, 4
HALF = GY // 2
VLIM = 52 << 20
MESH = pl.DeviceIdType.MESH
TABLE_ROWS = (256, 512, 256, 256, 256, 256, 256, 256, 256, 1024, 1024, 256)
FIRST_ROWS = sum(TABLE_ROWS[:5])
LATER_ROWS = sum(TABLE_ROWS[5:])
BF = jnp.bfloat16
F32 = jnp.float32


def dft_tables(length):
    indices = np.arange(length, dtype=np.int64)
    modular = indices[:, None] * indices[None, :] % length
    angles = modular.astype(np.float32) * np.float32(2.0 * math.pi / length)
    factor = np.float32(1.0 / math.sqrt(length))
    return tuple(
        (f(angles) * factor).astype(ml_dtypes.bfloat16).astype(np.float32)
        for f in (np.cos, np.sin)
    )


def complex_forward(c, s):
    m = np.zeros((c.shape[0], 2, c.shape[1], 2), np.float32)
    m[:, 0, :, 0], m[:, 0, :, 1] = c, s
    m[:, 1, :, 1], m[:, 1, :, 0] = c, -s
    return m


def real_pair_forward(c, s):
    n = c.shape[0]
    m = np.zeros((n, 2, n, 2), np.float32)
    for part in (0, 1):
        base = part * (n // 2)
        m[base, 0, :, part], m[base, 1, :, part] = c[0], c[n // 2]
        m[base + 1 : base + n // 2, 0, :, part] = c[1 : n // 2]
        m[base + 1 : base + n // 2, 1, :, part] = -s[1 : n // 2]
    return m


def line_pair_forward(c, s):
    n = c.shape[0]
    m = real_pair_forward(c, s)
    m[0], m[n // 2] = 0.0, 0.0
    for part in (0, 1):
        m[0, part, :, part] = c[0]
        m[n // 2, part, :, part] = c[n // 2]
    return m


def complex_inverse(c, s):
    m = np.zeros((c.shape[0], 2, c.shape[1], 2), np.float32)
    m[:, 0, :, 0], m[:, 0, :, 1] = c, -s
    m[:, 1, :, 1], m[:, 1, :, 0] = c, s
    return m


def doubled(forward):
    m = np.transpose(forward, (2, 3, 0, 1)).copy()
    n = m.shape[2]
    m[:, :, 1 : n // 2] *= 2.0
    m[:, :, n // 2 + 1 :] *= 2.0
    return m


@functools.cache
def constants():
    cx, sx = dft_tables(GX)
    cy, sy = dft_tables(GY)
    cz, sz = dft_tables(GZ)
    to_y = np.concatenate([cy[:, :HALF], -sy[:, :HALF]], axis=1)
    to_y[:, HALF] = cy[:, HALF]
    pool = np.repeat(0.5 * np.eye(GY, dtype=np.float32), 2, axis=0)
    eye4, eye8 = np.eye(4, dtype=np.float32), np.eye(8, dtype=np.float32)

    split = np.zeros((2, 4, GX, 4, GX, 2), np.float32)
    for parity in (0, 1):
        split[parity, ..., parity] = np.einsum("zw,xv->zxwv", eye4, np.eye(GX, dtype=np.float32))

    def x_forward(m):
        return np.einsum("kpxq,zw->kpzqwx", m, eye4).reshape(256, 256)

    def z_forward(m):
        m = m.reshape(32, 4, 2, 8, 4, 4, 2)
        return np.transpose(m, (0, 2, 1, 3, 4, 6, 5)).reshape(256, 256)

    def z_inverse(m):
        m = m.reshape(8, 4, 4, 2, 32, 4, 2)
        return np.transpose(m, (0, 1, 3, 2, 4, 6, 5)).reshape(256, 256)

    def x_inverse(m):
        e = eye8.reshape(8, 2, 4)
        m = np.einsum("xpkq,zgw->pzxkgqw", m, e).reshape(512, 8, 2, 32)
        return np.transpose(m, (0, 2, 1, 3)).reshape(512, 512)

    from_y = np.concatenate([2.0 * cy[:HALF], -2.0 * sy[:HALF]], axis=0)
    from_y[0], from_y[HALF] = cy[0], cy[HALF]
    z_line = line_pair_forward(cz, sz)
    x_line = real_pair_forward(cx, sx)
    tables = (
        split.reshape(256, 256),
        pool,
        to_y,
        x_forward(complex_forward(cx, sx)),
        x_forward(x_line),
        z_forward(complex_forward(cz, sz)),
        z_forward(z_line),
        z_inverse(complex_inverse(cz, sz)),
        z_inverse(doubled(z_line)),
        x_inverse(complex_inverse(cx, sx)),
        x_inverse(doubled(x_line)),
        from_y,
    )
    tables = [t.reshape(-1, 256) if t.shape[1] == 256 else np.concatenate([t[:, :256], t[:, 256:]]) for t in tables]
    return np.concatenate(tables).astype(ml_dtypes.bfloat16)


def dot(a, b):
    return jnp.dot(a, b, preferred_element_type=F32)


def body(tiles, slabs, *refs):
    (pairs_hbm, extents_hbm, band, hbm_tables, out, raw, tables, pairs_v, extents_v, *rest) = refs
    s1, r1, s2, r2_first, r2_second, s3, r3, s4, r4, pairs_s, raw_sem, table_sem, *sems = rest
    send1, recv1, send2, recv2, send3, recv3, send4, recv4 = sems
    at, views = 0, []
    for rows in TABLE_ROWS:
        views.append(tables.at[pl.ds(at, rows)])
        at += rows
    r2 = (r2_first, r2_second)
    split, pool, to_y, xf, xf0, zf, zf0, zi, zi0, xi, xi0, from_y = views
    t = lax.axis_index("tile")
    s = lax.axis_index("zslab")

    barrier = pltpu.get_barrier_semaphore()

    @pl.loop(1, slabs)
    def _(i):
        pl.semaphore_signal(
            barrier, inc=1, device_id=(t, lax.rem(s + i, slabs)), device_id_type=MESH
        )

    @pl.loop(1, tiles)
    def _(i):
        pl.semaphore_signal(
            barrier, inc=1, device_id=(lax.rem(t + i, tiles), s), device_id_type=MESH
        )

    fetches = [
        pltpu.make_async_copy(
            hbm_tables.at[pl.ds(0, FIRST_ROWS)], tables.at[pl.ds(0, FIRST_ROWS)], table_sem.at[0]
        ),
        pltpu.make_async_copy(pairs_hbm, pairs_v, table_sem.at[1]),
        pltpu.make_async_copy(extents_hbm, extents_v, table_sem.at[2]),
    ]
    later = pltpu.make_async_copy(
        hbm_tables.at[pl.ds(FIRST_ROWS, LATER_ROWS)],
        tables.at[pl.ds(FIRST_ROWS, LATER_ROWS)],
        table_sem.at[3],
    )
    for fetch in fetches:
        fetch.start()
    for f in range(FACES):
        pltpu.make_async_copy(band.at[f], raw.at[f], raw_sem.at[f]).start()
    later.start()
    index = pltpu.make_async_copy(pairs_hbm, pairs_s, table_sem.at[4])
    index.start()

    def slab_send(src, dst, send_sem, recv_sem):
        @pl.loop(1, slabs)
        def _(i):
            d = lax.rem(s + i, slabs)
            pltpu.make_async_remote_copy(
                src_ref=src.at[d],
                dst_ref=dst.at[s],
                send_sem=send_sem,
                recv_sem=recv_sem,
                device_id=(t, d),
                device_id_type=MESH,
            ).start()

        pltpu.make_async_copy(src.at[s], dst.at[s], recv_sem).start()

    def tile_send(src, dst, send_sem, recv_sem):
        @pl.loop(1, tiles)
        def _(i):
            d = lax.rem(t + i, tiles)
            pltpu.make_async_remote_copy(
                src_ref=src.at[d],
                dst_ref=dst.at[t],
                send_sem=send_sem,
                recv_sem=recv_sem,
                device_id=(d, s),
                device_id_type=MESH,
            ).start()

        pltpu.make_async_copy(src.at[t], dst.at[t], recv_sem).start()

    def wait_for(ref, sem):
        pltpu.make_async_copy(ref, ref, sem).wait()

    lane0 = lax.broadcasted_iota(jnp.int32, (256, 128), 1) == 0
    two_lane0 = lax.broadcasted_iota(jnp.int32, (256, 256), 1) % 128 == 0
    mixed_line = (s == 0) | (s == slabs // 2)

    for fetch in fetches:
        fetch.wait()
    first = pairs_v[0:1] * FACES + pairs_v[1:2]
    second = pairs_v[2:3] * FACES + pairs_v[3:4]
    y_rows = lax.broadcasted_iota(jnp.int32, (512, 256), 0)
    x_lanes = lax.broadcasted_iota(jnp.int32, (256, 256), 1) % 64


    def to_x(f):
        slot = t * FACES + f
        named = (first == slot) | (second == slot)
        ex = jnp.sum(jnp.where(named, extents_v[0:1], 0), axis=1, keepdims=True)
        ey = jnp.sum(jnp.where(named, extents_v[1:2], 0), axis=1, keepdims=True)
        y_pool = jnp.where(y_rows < ey, pool[...].astype(F32), 0.0).astype(BF)
        x_split = jnp.where(x_lanes < ex, split[...].astype(F32), 0.0).astype(BF)
        pltpu.make_async_copy(band.at[f], raw.at[f], raw_sem.at[f]).wait()
        parts = []
        for half in range(2):
            y = []
            for g in range(2):
                rows = raw[f, pl.ds(512 * half + 256 * g, 256), :]
                parted = dot(x_split, rows).astype(BF)
                down = (dot(parted[:128], y_pool) + dot(parted[128:], y_pool)).astype(BF)
                y.append(dot(down, to_y[...]).astype(BF))
            stacked = jnp.concatenate(
                [
                    jnp.concatenate([y[0][:, :128], y[1][:, :128]], axis=1),
                    jnp.concatenate([y[0][:, 128:], y[1][:, 128:]], axis=1),
                ],
                axis=0,
            )
            x = jnp.where(two_lane0, dot(xf0[...], stacked), dot(xf[...], stacked))
            parts += [x[:, :128].reshape(32, 8, 128), x[:, 128:].reshape(32, 8, 128)]
        whole = jnp.concatenate(parts, axis=1).astype(BF)
        whole = whole.reshape(slabs, 2, 2, 32, 128)
        for h in range(2):
            s1[h, f] = whole[:, h]

    def mix_tables():
        later.wait()
        index.wait()
        zf0[...] = jnp.where(mixed_line, zf0[...].astype(F32), zf[...].astype(F32)).astype(BF)
        zi0[...] = jnp.where(mixed_line, zi0[...].astype(F32), zi[...].astype(F32)).astype(BF)

    def to_z(h, f):
        wait_for(r1.at[h, f], recv1.at[h, f])
        blocks = [r1[h, f, :, k].reshape(256, 128) for k in range(2)]
        z = dot(zf[...], jnp.concatenate(blocks, axis=1))
        parts = [z[:, :128], z[:, 128:]]
        if h == 0:
            parts[0] = jnp.where(lane0, dot(zf0[...], blocks[0]), parts[0])
        parts = [p.reshape(tiles, 8, 128) for p in parts]
        s2[h, f] = jnp.concatenate(parts, axis=1).astype(BF)
        tile_send(s2.at[h, f], r2[h].at[f], send2.at[h, f], recv2.at[h, f])

    def send_slot(h, f):
        slab_send(s1.at[h, f], r1.at[h, f], send1.at[h, f], recv1.at[h, f])

    def forward(i, carry):
        @pl.when(i < FACES)
        def _():
            to_x(i)

            @pl.when(i == 0)
            def _():
                pl.semaphore_wait(barrier, slabs - 1 + tiles - 1)

            send_slot(0, i)

            @pl.when(i == 0)
            def _():
                mix_tables()

        @pl.when(i > 0)
        def _():
            to_z(0, i - 1)
            send_slot(1, i - 1)

        return carry

    lax.fori_loop(0, FACES + 1, forward, 0)

    def forward_rest(f, carry):
        to_z(1, f)
        return carry

    lax.fori_loop(0, FACES, forward_rest, 0)

    row = lax.broadcasted_iota(jnp.int32, (8, 128), 0)
    lane = lax.broadcasted_iota(jnp.int32, (8, 128), 1)
    mixed_here = mixed_line & ((t == 0) | (t == tiles // 2))
    two_reals = (lane == 0) & (lax.rem(row, 4) == 0) & mixed_here
    real_row = row < 4

    def cross_half(h):
        for f in range(FACES):
            wait_for(r2[h].at[f], recv2.at[h, f])

        def correlate(i, carry):
            q = lax.div(i, tiles)
            d = lax.rem(t + 1 + i, tiles)
            p = 2 * d + q
            a = r2[h][pairs_s[1, p], pairs_s[0, p]].astype(F32)
            b = r2[h][pairs_s[3, p], pairs_s[2, p]].astype(F32)
            parts = []
            for k in range(2):
                ak, bk = a[8 * k : 8 * k + 8], b[8 * k : 8 * k + 8]
                same = ak * bk
                turned = pltpu.roll(ak, 4, axis=0) * bk
                cross = jnp.where(
                    real_row,
                    same + pltpu.roll(same, 4, axis=0),
                    pltpu.roll(turned, 4, axis=0) - turned,
                )
                mixed = h == 0 and k == 0
                if mixed:
                    cross = jnp.where(two_reals, same, cross)
                square = cross * cross
                total = square + pltpu.roll(square, 4, axis=0)
                if mixed:
                    total = jnp.where(two_reals, square, total)
                parts.append(cross * lax.rsqrt(total + 1.0))
            s3[h, q, d] = jnp.concatenate(parts, axis=0).astype(BF)

            @pl.when(lax.rem(i, tiles) < tiles - 1)
            def _():
                pltpu.make_async_remote_copy(
                    src_ref=s3.at[h, q, d],
                    dst_ref=r3.at[h, q, t],
                    send_sem=send3.at[h, q],
                    recv_sem=recv3.at[h, q],
                    device_id=(d, s),
                    device_id_type=MESH,
                ).start()

            return carry

        lax.fori_loop(0, 2 * tiles, correlate, 0)
        for q in range(2):
            pltpu.make_async_copy(s3.at[h, q, t], r3.at[h, q, t], recv3.at[h, q]).start()

    cross_half(0)
    cross_half(1)

    def from_z(h, q):
        wait_for(r3.at[h, q], recv3.at[h, q])
        got = r3[h, q].astype(F32)
        blocks = [got[:, 8 * k : 8 * k + 8].reshape(256, 128).astype(BF) for k in range(2)]
        w = dot(zi[...], jnp.concatenate(blocks, axis=1))
        parts = [w[:, :128], w[:, 128:]]
        if h == 0:
            parts[0] = jnp.where(lane0, dot(zi0[...], blocks[0]), parts[0])
        for k in range(2):
            s4[h, q, :, k] = parts[k].astype(BF).reshape(slabs, 32, 128)
        slab_send(s4.at[h, q], r4.at[h, q], send4.at[h, q], recv4.at[h, q])

    for h in range(2):
        for q in range(2):
            from_z(h, q)

    def from_x(q, carry):
        for h in range(2):
            wait_for(r4.at[h, q], recv4.at[h, q])
        for half in range(2):
            blocks = [
                r4[h, q, :, :, pl.ds(16 * half, 16), :].reshape(256, 128) for h in range(2)
            ]
            v = dot(xi[:512], blocks[0]) + dot(xi[512:], blocks[1])
            v0 = dot(xi0[:512], blocks[0]) + dot(xi0[512:], blocks[1])
            re = jnp.where(lane0, v0[:256], v[:256]).astype(BF)
            im = jnp.where(lane0, v0[256:], v[256:]).astype(BF)
            out[q, pl.ds(256 * half, 256), :] = dot(
                jnp.concatenate([re, im], axis=1), from_y[...]
            )
        return carry

    lax.fori_loop(0, 2, from_x, 0)

    for h in range(2):
        for f in range(FACES):
            wait_for(s1.at[h, f, pl.ds(0, slabs - 1)], send1.at[h, f])
            wait_for(s2.at[h, f, pl.ds(0, tiles - 1)], send2.at[h, f])
        for q in range(2):
            wait_for(s3.at[h, q, pl.ds(0, tiles - 1)], send3.at[h, q])
            wait_for(s4.at[h, q, pl.ds(0, slabs - 1)], send4.at[h, q])


def solution(mesh):
    tiles, slabs = mesh.shape["tile"], mesh.shape["zslab"]

    def shards(band, pairs, extents):
        tables = constants()
        vmem = pl.BlockSpec(memory_space=pltpu.VMEM)
        hbm = pl.BlockSpec(memory_space=pltpu.HBM)
        dma = pltpu.SemaphoreType.DMA
        scratch = [pltpu.VMEM((FACES, 1024, 512), BF)]
        scratch += [pltpu.VMEM(tables.shape, BF)]
        scratch += [pltpu.VMEM((4, 64), jnp.int32), pltpu.VMEM((2, 64), jnp.int32)]
        scratch += [pltpu.VMEM((2, FACES, slabs, 2, 32, 128), BF)] * 2
        scratch += [pltpu.VMEM((2, FACES, tiles, 16, 128), BF)]
        scratch += [pltpu.VMEM((FACES, tiles, 16, 128), BF)] * 2
        scratch += [pltpu.VMEM((2, 2, tiles, 16, 128), BF)] * 2
        scratch += [pltpu.VMEM((2, 2, slabs, 2, 32, 128), BF)] * 2
        scratch += [pltpu.SMEM((4, 64), jnp.int32), dma((FACES,)), dma((5,))]
        scratch += [dma((2, FACES))] * 4 + [dma((2, 2))] * 4
        maps = pl.pallas_call(
            functools.partial(body, tiles, slabs),
            out_shape=jax.ShapeDtypeStruct((2, 512, 256), F32),
            in_specs=[hbm] * 4,
            out_specs=vmem,
            scratch_shapes=scratch,
            compiler_params=pltpu.CompilerParams(
                collective_id=0, has_side_effects=True, vmem_limit_bytes=VLIM
            ),
        )(pltpu.with_memory_space_constraint(pairs.T, pltpu.HBM), pltpu.with_memory_space_constraint(extents.T, pltpu.HBM), band.reshape(FACES, 1024, 512), tables)
        return maps.reshape(2, 16, GX, GY)

    placed = (P("tile", None, "zslab", None, None), P(), P())
    return jax.shard_map(
        shards,
        mesh=mesh,
        in_specs=placed,
        out_specs=P("tile", "zslab", None, None),
        check_vma=False,
    )
```

```python
import functools
import math

import jax
import jax.numpy as jnp
import ml_dtypes
import numpy as np
from jax import lax
from jax.experimental import pallas as pl
from jax.experimental.pallas import tpu as pltpu
from jax.sharding import PartitionSpec as P

GX, GY, GZ, FACES = 32, 256, 128, 4
HALF = GY // 2
VLIM = 52 << 20
MESH = pl.DeviceIdType.MESH
TABLE_ROWS = (512, 256, 256, 256, 256, 256, 256, 256, 1024, 1024, 256)
FIRST_ROWS = sum(TABLE_ROWS[:4])
LATER_ROWS = sum(TABLE_ROWS[4:])
BF = jnp.bfloat16
F32 = jnp.float32


def dft_tables(length):
    indices = np.arange(length, dtype=np.int64)
    modular = indices[:, None] * indices[None, :] % length
    angles = modular.astype(np.float32) * np.float32(2.0 * math.pi / length)
    factor = np.float32(1.0 / math.sqrt(length))
    return tuple(
        (f(angles) * factor).astype(ml_dtypes.bfloat16).astype(np.float32)
        for f in (np.cos, np.sin)
    )


def complex_forward(c, s):
    m = np.zeros((c.shape[0], 2, c.shape[1], 2), np.float32)
    m[:, 0, :, 0], m[:, 0, :, 1] = c, s
    m[:, 1, :, 1], m[:, 1, :, 0] = c, -s
    return m


def real_pair_forward(c, s):
    n = c.shape[0]
    m = np.zeros((n, 2, n, 2), np.float32)
    for part in (0, 1):
        base = part * (n // 2)
        m[base, 0, :, part], m[base, 1, :, part] = c[0], c[n // 2]
        m[base + 1 : base + n // 2, 0, :, part] = c[1 : n // 2]
        m[base + 1 : base + n // 2, 1, :, part] = -s[1 : n // 2]
    return m


def line_pair_forward(c, s):
    n = c.shape[0]
    m = real_pair_forward(c, s)
    m[0], m[n // 2] = 0.0, 0.0
    for part in (0, 1):
        m[0, part, :, part] = c[0]
        m[n // 2, part, :, part] = c[n // 2]
    return m


def complex_inverse(c, s):
    m = np.zeros((c.shape[0], 2, c.shape[1], 2), np.float32)
    m[:, 0, :, 0], m[:, 0, :, 1] = c, -s
    m[:, 1, :, 1], m[:, 1, :, 0] = c, s
    return m


def doubled(forward):
    m = np.transpose(forward, (2, 3, 0, 1)).copy()
    n = m.shape[2]
    m[:, :, 1 : n // 2] *= 2.0
    m[:, :, n // 2 + 1 :] *= 2.0
    return m


@functools.cache
def constants():
    cx, sx = dft_tables(GX)
    cy, sy = dft_tables(GY)
    cz, sz = dft_tables(GZ)
    to_y = np.concatenate([cy[:, :HALF], -sy[:, :HALF]], axis=1)
    to_y[:, HALF] = cy[:, HALF]
    pool = np.repeat(0.5 * np.eye(GY, dtype=np.float32), 2, axis=0)
    eye4, eye8 = np.eye(4, dtype=np.float32), np.eye(8, dtype=np.float32)

    def x_forward(m):
        return np.einsum("kpxq,zw->kpzqwx", m, eye4).reshape(256, 256)

    def z_forward(m):
        m = m.reshape(32, 4, 2, 8, 4, 4, 2)
        return np.transpose(m, (0, 2, 1, 3, 4, 6, 5)).reshape(256, 256)

    def z_inverse(m):
        m = m.reshape(8, 4, 4, 2, 32, 4, 2)
        return np.transpose(m, (0, 1, 3, 2, 4, 6, 5)).reshape(256, 256)

    def x_inverse(m):
        e = eye8.reshape(8, 2, 4)
        m = np.einsum("xpkq,zgw->pzxkgqw", m, e).reshape(512, 8, 2, 32)
        return np.transpose(m, (0, 2, 1, 3)).reshape(512, 512)

    from_y = np.concatenate([2.0 * cy[:HALF], -2.0 * sy[:HALF]], axis=0)
    from_y[0], from_y[HALF] = cy[0], cy[HALF]
    z_line = line_pair_forward(cz, sz)
    x_line = real_pair_forward(cx, sx)
    tables = (
        pool,
        to_y,
        x_forward(complex_forward(cx, sx)),
        x_forward(x_line),
        z_forward(complex_forward(cz, sz)),
        z_forward(z_line),
        z_inverse(complex_inverse(cz, sz)),
        z_inverse(doubled(z_line)),
        x_inverse(complex_inverse(cx, sx)),
        x_inverse(doubled(x_line)),
        from_y,
    )
    tables = [t.reshape(-1, 256) if t.shape[1] == 256 else np.concatenate([t[:, :256], t[:, 256:]]) for t in tables]
    return np.concatenate(tables).astype(ml_dtypes.bfloat16)


def dot(a, b):
    return jnp.dot(a, b, preferred_element_type=F32)


def body(tiles, slabs, *refs):
    (pairs_hbm, extents_hbm, band, hbm_tables, out, raw, tables, pairs_v, extents_v, *rest) = refs
    s1, r1, s2, r2_first, r2_second, s3, r3, s4, r4, pairs_s, halved, partial, raw_sem, table_sem, *sems = rest
    send1, recv1, send2, recv2, send3, recv3, send4, recv4 = sems
    at, views = 0, []
    for rows in TABLE_ROWS:
        views.append(tables.at[pl.ds(at, rows)])
        at += rows
    r2 = (r2_first, r2_second)
    pool, to_y, xf, xf0, zf, zf0, zi, zi0, xi, xi0, from_y = views
    t = lax.axis_index("tile")
    s = lax.axis_index("zslab")

    barrier = pltpu.get_barrier_semaphore()

    @pl.loop(1, slabs)
    def _(i):
        pl.semaphore_signal(
            barrier, inc=1, device_id=(t, lax.rem(s + i, slabs)), device_id_type=MESH
        )

    @pl.loop(1, tiles)
    def _(i):
        pl.semaphore_signal(
            barrier, inc=1, device_id=(lax.rem(t + i, tiles), s), device_id_type=MESH
        )

    fetches = [
        pltpu.make_async_copy(
            hbm_tables.at[pl.ds(0, FIRST_ROWS)], tables.at[pl.ds(0, FIRST_ROWS)], table_sem.at[0]
        ),
        pltpu.make_async_copy(pairs_hbm, pairs_v, table_sem.at[1]),
        pltpu.make_async_copy(extents_hbm, extents_v, table_sem.at[2]),
    ]
    later = pltpu.make_async_copy(
        hbm_tables.at[pl.ds(FIRST_ROWS, LATER_ROWS)],
        tables.at[pl.ds(FIRST_ROWS, LATER_ROWS)],
        table_sem.at[3],
    )
    for fetch in fetches:
        fetch.start()
    for f in range(FACES):
        pltpu.make_async_copy(band.at[f], raw.at[f], raw_sem.at[f]).start()
    later.start()
    index = pltpu.make_async_copy(pairs_hbm, pairs_s, table_sem.at[4])
    index.start()

    def slab_send(src, dst, send_sem, recv_sem):
        @pl.loop(1, slabs)
        def _(i):
            d = lax.rem(s + i, slabs)
            pltpu.make_async_remote_copy(
                src_ref=src.at[d],
                dst_ref=dst.at[s],
                send_sem=send_sem,
                recv_sem=recv_sem,
                device_id=(t, d),
                device_id_type=MESH,
            ).start()

        pltpu.make_async_copy(src.at[s], dst.at[s], recv_sem).start()

    def tile_send(src, dst, send_sem, recv_sem):
        @pl.loop(1, tiles)
        def _(i):
            d = lax.rem(t + i, tiles)
            pltpu.make_async_remote_copy(
                src_ref=src.at[d],
                dst_ref=dst.at[t],
                send_sem=send_sem,
                recv_sem=recv_sem,
                device_id=(d, s),
                device_id_type=MESH,
            ).start()

        pltpu.make_async_copy(src.at[t], dst.at[t], recv_sem).start()

    def wait_for(ref, sem):
        pltpu.make_async_copy(ref, ref, sem).wait()

    lane0 = lax.broadcasted_iota(jnp.int32, (256, 128), 1) == 0
    two_lane0 = lax.broadcasted_iota(jnp.int32, (256, 256), 1) % 128 == 0
    wide_lane0 = lax.broadcasted_iota(jnp.int32, (512, 128), 1) == 0
    mixed_line = (s == 0) | (s == slabs // 2)

    for fetch in fetches:
        fetch.wait()
    first = pairs_v[0:1] * FACES + pairs_v[1:2]
    second = pairs_v[2:3] * FACES + pairs_v[3:4]
    y_rows = lax.broadcasted_iota(jnp.int32, (512, 256), 0)
    x_even = lax.broadcasted_iota(jnp.int32, (128, 256), 0) % 32 * 2


    def to_x(f):
        slot = t * FACES + f
        named = (first == slot) | (second == slot)
        ex = jnp.sum(jnp.where(named, extents_v[0:1], 0), axis=1, keepdims=True)
        ey = jnp.sum(jnp.where(named, extents_v[1:2], 0), axis=1, keepdims=True)
        y_pool = jnp.where(y_rows < ey, pool[...].astype(F32), 0.0).astype(BF)
        even_live, odd_live = x_even < ex, x_even + 1 < ex
        pltpu.make_async_copy(band.at[f], raw.at[f], raw_sem.at[f]).wait()
        parts = []
        for half in range(2):
            y = []
            for g in range(2):
                rows = raw[f, pl.ds(512 * half + 256 * g, 256), :]
                summed = dot(rows, y_pool)
                even, odd = [], []
                for w in range(2):
                    halved[half, g, w] = summed[:, 128 * w : 128 * w + 128]
                    even.append(halved[half, g, w, pl.ds(0, 128, stride=2), :])
                    odd.append(halved[half, g, w, pl.ds(1, 128, stride=2), :])
                even = jnp.where(even_live, jnp.concatenate(even, axis=1), 0.0)
                odd = jnp.where(odd_live, jnp.concatenate(odd, axis=1), 0.0)
                down = (even + odd).astype(BF)
                y.append(dot(down, to_y[...]).astype(BF))
            stacked = jnp.concatenate(
                [
                    jnp.concatenate([y[0][:, :128], y[1][:, :128]], axis=1),
                    jnp.concatenate([y[0][:, 128:], y[1][:, 128:]], axis=1),
                ],
                axis=0,
            )
            x = jnp.where(two_lane0, dot(xf0[...], stacked), dot(xf[...], stacked))
            parts += [x[:, :128].reshape(32, 8, 128), x[:, 128:].reshape(32, 8, 128)]
        whole = jnp.concatenate(parts, axis=1).astype(BF)
        whole = whole.reshape(slabs, 2, 2, 32, 128)
        for h in range(2):
            s1[h, f] = whole[:, h]

    def mix_tables():
        later.wait()
        index.wait()
        zf0[...] = jnp.where(mixed_line, zf0[...].astype(F32), zf[...].astype(F32)).astype(BF)
        zi0[...] = jnp.where(mixed_line, zi0[...].astype(F32), zi[...].astype(F32)).astype(BF)

    def to_z(h, f):
        wait_for(r1.at[h, f], recv1.at[h, f])
        blocks = [r1[h, f, :, k].reshape(256, 128) for k in range(2)]
        z = dot(zf[...], jnp.concatenate(blocks, axis=1))
        parts = [z[:, :128], z[:, 128:]]
        if h == 0:
            parts[0] = jnp.where(lane0, dot(zf0[...], blocks[0]), parts[0])
        parts = [p.reshape(tiles, 8, 128) for p in parts]
        s2[h, f] = jnp.concatenate(parts, axis=1).astype(BF)
        tile_send(s2.at[h, f], r2[h].at[f], send2.at[h, f], recv2.at[h, f])

    def send_slot(h, f):
        slab_send(s1.at[h, f], r1.at[h, f], send1.at[h, f], recv1.at[h, f])

    def forward(i, carry):
        @pl.when(i < FACES)
        def _():
            to_x(i)

            @pl.when(i == 0)
            def _():
                pl.semaphore_wait(barrier, slabs - 1 + tiles - 1)

            send_slot(0, i)

            @pl.when(i == 0)
            def _():
                mix_tables()

        @pl.when(i > 0)
        def _():
            to_z(0, i - 1)
            send_slot(1, i - 1)

        return carry

    lax.fori_loop(0, FACES + 1, forward, 0)

    def forward_rest(f, carry):
        to_z(1, f)
        return carry

    lax.fori_loop(0, FACES, forward_rest, 0)

    row = lax.broadcasted_iota(jnp.int32, (8, 128), 0)
    lane = lax.broadcasted_iota(jnp.int32, (8, 128), 1)
    mixed_here = mixed_line & ((t == 0) | (t == tiles // 2))
    two_reals = (lane == 0) & (lax.rem(row, 4) == 0) & mixed_here
    real_row = row < 4

    def cross_half(h):
        for f in range(FACES):
            wait_for(r2[h].at[f], recv2.at[h, f])

        def correlate(i, carry):
            q = lax.div(i, tiles)
            d = lax.rem(t + 1 + i, tiles)
            p = 2 * d + q
            a = r2[h][pairs_s[1, p], pairs_s[0, p]].astype(F32)
            b = r2[h][pairs_s[3, p], pairs_s[2, p]].astype(F32)
            parts = []
            for k in range(2):
                ak, bk = a[8 * k : 8 * k + 8], b[8 * k : 8 * k + 8]
                same = ak * bk
                turned = pltpu.roll(ak, 4, axis=0) * bk
                cross = jnp.where(
                    real_row,
                    same + pltpu.roll(same, 4, axis=0),
                    pltpu.roll(turned, 4, axis=0) - turned,
                )
                mixed = h == 0 and k == 0
                if mixed:
                    cross = jnp.where(two_reals, same, cross)
                square = cross * cross
                total = square + pltpu.roll(square, 4, axis=0)
                if mixed:
                    total = jnp.where(two_reals, square, total)
                parts.append(cross * lax.rsqrt(total + 1.0))
            s3[h, q, d] = jnp.concatenate(parts, axis=0).astype(BF)

            @pl.when(lax.rem(i, tiles) < tiles - 1)
            def _():
                pltpu.make_async_remote_copy(
                    src_ref=s3.at[h, q, d],
                    dst_ref=r3.at[h, q, t],
                    send_sem=send3.at[h, q],
                    recv_sem=recv3.at[h, q],
                    device_id=(d, s),
                    device_id_type=MESH,
                ).start()

            return carry

        lax.fori_loop(0, 2 * tiles, correlate, 0)
        for q in range(2):
            pltpu.make_async_copy(s3.at[h, q, t], r3.at[h, q, t], recv3.at[h, q]).start()

    cross_half(0)
    cross_half(1)

    def from_z(h, q):
        wait_for(r3.at[h, q], recv3.at[h, q])
        got = r3[h, q].astype(F32)
        blocks = [got[:, 8 * k : 8 * k + 8].reshape(256, 128).astype(BF) for k in range(2)]
        w = dot(zi[...], jnp.concatenate(blocks, axis=1))
        parts = [w[:, :128], w[:, 128:]]
        if h == 0:
            parts[0] = jnp.where(lane0, dot(zi0[...], blocks[0]), parts[0])
        for k in range(2):
            s4[h, q, :, k] = parts[k].astype(BF).reshape(slabs, 32, 128)
        slab_send(s4.at[h, q], r4.at[h, q], send4.at[h, q], recv4.at[h, q])

    def from_x(h, q):
        wait_for(r4.at[h, q], recv4.at[h, q])
        for half in range(2):
            block = r4[h, q, :, :, pl.ds(16 * half, 16), :].reshape(256, 128)
            rows = pl.ds(512 * h, 512)
            v = jnp.where(wide_lane0, dot(xi0[rows], block), dot(xi[rows], block))
            if h == 0:
                partial[q, half] = v
                continue
            v = (partial[q, half] + v).astype(BF)
            out[q, pl.ds(256 * half, 256), :] = dot(
                jnp.concatenate([v[:256], v[256:]], axis=1), from_y[...]
            )

    for h in range(2):
        for q in range(2):
            from_z(h, q)
        for q in range(2):
            from_x(h, q)

    for h in range(2):
        for f in range(FACES):
            wait_for(s1.at[h, f, pl.ds(0, slabs - 1)], send1.at[h, f])
            wait_for(s2.at[h, f, pl.ds(0, tiles - 1)], send2.at[h, f])
        for q in range(2):
            wait_for(s3.at[h, q, pl.ds(0, tiles - 1)], send3.at[h, q])
            wait_for(s4.at[h, q, pl.ds(0, slabs - 1)], send4.at[h, q])


def solution(mesh):
    tiles, slabs = mesh.shape["tile"], mesh.shape["zslab"]

    def shards(band, pairs, extents):
        tables = constants()
        vmem = pl.BlockSpec(memory_space=pltpu.VMEM)
        hbm = pl.BlockSpec(memory_space=pltpu.HBM)
        dma = pltpu.SemaphoreType.DMA
        scratch = [pltpu.VMEM((FACES, 1024, 512), BF)]
        scratch += [pltpu.VMEM(tables.shape, BF)]
        scratch += [pltpu.VMEM((4, 64), jnp.int32), pltpu.VMEM((2, 64), jnp.int32)]
        scratch += [pltpu.VMEM((2, FACES, slabs, 2, 32, 128), BF)] * 2
        scratch += [pltpu.VMEM((2, FACES, tiles, 16, 128), BF)]
        scratch += [pltpu.VMEM((FACES, tiles, 16, 128), BF)] * 2
        scratch += [pltpu.VMEM((2, 2, tiles, 16, 128), BF)] * 2
        scratch += [pltpu.VMEM((2, 2, slabs, 2, 32, 128), BF)] * 2
        scratch += [pltpu.SMEM((4, 64), jnp.int32), pltpu.VMEM((2, 2, 2, 256, 128), F32), pltpu.VMEM((2, 2, 512, 128), F32), dma((FACES,)), dma((5,))]
        scratch += [dma((2, FACES))] * 4 + [dma((2, 2))] * 4
        maps = pl.pallas_call(
            functools.partial(body, tiles, slabs),
            out_shape=jax.ShapeDtypeStruct((2, 512, 256), F32),
            in_specs=[hbm] * 4,
            out_specs=vmem,
            scratch_shapes=scratch,
            compiler_params=pltpu.CompilerParams(
                collective_id=0, has_side_effects=True, vmem_limit_bytes=VLIM
            ),
        )(pltpu.with_memory_space_constraint(pairs.T, pltpu.HBM), pltpu.with_memory_space_constraint(extents.T, pltpu.HBM), band.reshape(FACES, 1024, 512), tables)
        return maps.reshape(2, 16, GX, GY)

    placed = (P("tile", None, "zslab", None, None), P(), P())
    return jax.shard_map(
        shards,
        mesh=mesh,
        in_specs=placed,
        out_specs=P("tile", "zslab", None, None),
        check_vma=False,
    )
```
